32 devices in a mesh: wide: 4 (over x, core), rep: 8 (over z, y).
Axes of the slice: x: 2, y: 2, z: 4, core: 2. Of those that a mesh axis runs over, the one named last changes fastest.
Arguments:
- stretch_qkv: bfloat16 [8, 1536, 3, 5120], P('rep', 'wide'), may hold values from -60 to 60
- norm_gains: float32 [2, 5120], replicated, may hold values from 0.25 to 1.75
- cache: bfloat16 [128, 2, 192, 5120], P('rep', None, 'wide'), may hold values from -6 to 6
- cached_stretches: int32 [8], replicated, may hold values from 1 to 2, as said below
- block_slot: int32 [8, 16], replicated, may hold values from 0 to 127, as said below
- video_of_group: int32 [8], replicated, may hold values from 0 to 7, each once
Outputs:
- attended: bfloat16 [8, 1536, 5120], P('rep', 'wide')
The draws below stay inside these ranges and needn't reach their ends.
Inputs may be any that keep to these rules, and one draw needn't show every extreme that they name: `cached_stretches`: each value is 1 to 2; some video has exactly 2. Block b of video u holds that video's cached tokens b * 192 to (b + 1) * 192 - 1, oldest first; it is cache row block_slot[u, b], owned by group block_slot[u, b] // 16. Every group owns exactly 2 blocks of every video; no two blocks share a row.
All inputs are finite; a program needn't handle non-finite values.
Results may differ from the reference program's by a relative error of at most 0.011.
Values may be sent and summed in bfloat16 or wider, within the bound.
No kernel may reach another device: no remote copies, remote signals or barrier semaphores. Data moves between devices by JAX's collectives and lax.ppermute only.
A program may use at most 192 MiB of HBM per device.

```python
import math
import jax
import jax.numpy as jnp
from jax import lax

D = 5120
HEADS = 40
HD = 128
MAXC = 2
STRETCH = 1536
BLK = 192
NBLK = 16
VIDEOS = 8
CAP = 2
SLOTS = 16
KEYS = 4608
N_REP = 8


def draw_stretch_qkv(key, part):
    subkeys = jax.random.split(key, 3)
    full_shape = (VIDEOS, STRETCH, 3, D)
    draws_base = jax.random.normal(subkeys[0], full_shape, jnp.float32)
    log_ten = math.log(10.0)
    column_scale = jnp.exp(log_ten * jax.random.uniform(subkeys[1], (1, 1, 1, D), jnp.float32))
    row_scale = jnp.exp(log_ten * jax.random.uniform(subkeys[2], (VIDEOS, STRETCH, 1, 1), jnp.float32))
    component = jnp.arange(3).reshape(1, 1, 3, 1)
    scaled = jnp.where(component < 2, draws_base * column_scale * row_scale, draws_base)
    return jnp.clip(scaled, -60.0, 60.0).astype(jnp.bfloat16)


def draw_cached_stretches(key, part):
    counts = jax.random.randint(key, (VIDEOS,), 1, MAXC + 1)
    forced = jax.random.randint(jax.random.fold_in(key, 7), (), 0, VIDEOS)
    return jnp.where(jnp.arange(VIDEOS) == forced, MAXC, counts).astype(jnp.int32)


def draw_block_slot(key, part):
    owner_key = jax.random.fold_in(key, 11)
    slot_key = jax.random.fold_in(key, 12)
    owner_order = jax.vmap(lambda subkey: jax.random.permutation(subkey, VIDEOS))(jax.random.split(owner_key, VIDEOS))
    slot_order = jax.vmap(lambda subkey: jax.random.permutation(subkey, VIDEOS))(jax.random.split(slot_key, VIDEOS))
    block_index = jnp.arange(NBLK)
    owner_group = owner_order[:, block_index % VIDEOS]
    within = (block_index // VIDEOS)[None, :]
    video_index = jnp.arange(VIDEOS)[:, None]
    rank_here = slot_order[owner_group, video_index]
    return (owner_group * SLOTS + rank_here * CAP + within).astype(jnp.int32)


def block_scale(key, extent, cuts, low, largest):
    factor_of = 1.0
    for axis_at, parts in cuts:
        steps = jax.random.uniform(jax.random.fold_in(jax.random.fold_in(key, 6), axis_at), (parts,), jnp.float32, low / len(cuts), largest / len(cuts))
        factor_of = factor_of * jnp.repeat(jnp.exp(steps), extent[axis_at] // parts).reshape((-1,) + (1,) * (len(extent) - 1 - axis_at))
    return factor_of


def bell_draw(own_key, extent, scale, limit, pieces=(), kind=jnp.bfloat16):
    result = jax.random.normal(own_key, extent, jnp.float32) * scale
    if len(pieces) > 0:
        result = block_scale(own_key, extent, pieces, -0.22, 0.18) * result
    return jnp.clip(result, min=-limit, max=limit).astype(kind)


def setup_inputs(seed: int = 0) -> dict:
    splits = jax.random.split(jax.random.key(seed), 7)
    stretch_qkv = draw_stretch_qkv(jax.random.fold_in(splits[6], 71), 0)
    norm_gains = jnp.clip(1.0 + 0.15 * jax.random.normal(splits[1], (2, D), jnp.float32), 0.25, 1.75)
    cache = bell_draw(splits[2], (N_REP * SLOTS, 2, BLK, D), 1.0, 6.0, ((0, 8), (2, 4)))
    cached_stretches = draw_cached_stretches(jax.random.fold_in(splits[6], 71), 0)
    block_slot = draw_block_slot(jax.random.fold_in(splits[6], 71), 0)
    video_of_group = jax.random.permutation(splits[5], VIDEOS).astype(jnp.int32)
    return {"stretch_qkv": stretch_qkv, "norm_gains": norm_gains, "cache": cache, "cached_stretches": cached_stretches, "block_slot": block_slot, "video_of_group": video_of_group}


epsilon = 1e-06

def normalize(stretch_rows, gains_row):
    widened = stretch_rows.astype(jnp.float32)
    mean_square = lax.optimization_barrier(jnp.mean(widened * widened, axis=-1, keepdims=True))
    return (widened * lax.rsqrt(mean_square + epsilon) * gains_row).astype(jnp.bfloat16)

def attend_block(query_rows, all_keys, all_values, usable):
    scores = jnp.einsum('qhd,khd->hqk', query_rows.astype(jnp.float32), all_keys.astype(jnp.float32)) * HD ** (-0.5)
    scores = jnp.where(usable[None, None, :], scores, -jnp.inf)
    row_max = lax.optimization_barrier(jnp.max(scores, axis=-1, keepdims=True))
    weights = jnp.exp(scores - row_max)
    row_total = lax.optimization_barrier(jnp.sum(weights, axis=-1, keepdims=True))
    rounded = lax.optimization_barrier(weights.astype(jnp.bfloat16)).astype(jnp.float32)
    mixed = jnp.einsum('hqk,khd->qhd', rounded, all_values.astype(jnp.float32))
    return (mixed / jnp.transpose(row_total, (1, 0, 2))).astype(jnp.bfloat16)

def reference(stretch_qkv, norm_gains, cache, cached_stretches, block_slot, video_of_group):
    query_block = math.gcd(STRETCH, 256)

    def one_group(group_index):
        own_video = video_of_group[group_index]
        stretch_rows = stretch_qkv[group_index]
        queries = normalize(stretch_rows[:, 0], norm_gains[0])
        keys_new = normalize(stretch_rows[:, 1], norm_gains[1])
        held_blocks = cache[block_slot[own_video]]
        all_keys = jnp.concatenate([held_blocks[:, 0].reshape(NBLK * BLK, D), keys_new], axis=0)
        all_values = jnp.concatenate([held_blocks[:, 1].reshape(NBLK * BLK, D), stretch_rows[:, 2]], axis=0)
        all_keys = all_keys.reshape(KEYS, HEADS, HD)
        all_values = all_values.reshape(KEYS, HEADS, HD)
        key_position = jnp.arange(KEYS, dtype=jnp.int32)
        usable = (key_position < cached_stretches[own_video] * STRETCH) | (key_position >= NBLK * BLK)
        blocks_q = queries.reshape(STRETCH // query_block, query_block, HEADS, HD)
        attended = lax.map(lambda piece: attend_block(piece, all_keys, all_values, usable), blocks_q)
        return attended.reshape(STRETCH, D)
    return lax.map(one_group, jnp.arange(VIDEOS, dtype=jnp.int32))
```

```python
import functools
import math

import jax
import jax.numpy as jnp
from jax import lax
from jax.experimental import pallas as pl
from jax.experimental.pallas import tpu as pltpu
from jax.sharding import Mesh, PartitionSpec as P

HD = 128
EPS = 1e-06
VMEM_LIMIT = 56 * 1024 * 1024
CHUNKS = (5, 8, 5, 2)


def pack_kernel(cap, head0, width, half, place_ref, slots_ref, videos_ref, cache_ref, out_ref, sems):
    own_group = place_ref[0]
    groups = videos_ref.shape[0]
    blocks = slots_ref.shape[1]
    slots_dev = cache_ref.shape[0]

    def copy_of(slot, group, rank, core):
        return pltpu.make_async_copy(
            cache_ref.at[slot, :, :, pl.ds(core * half + head0 * HD, width)],
            out_ref.at[core * groups + group, :, rank],
            sems.at[(group * cap + rank) * 2 + core],
        )

    def each_group(group, carry):
        video = videos_ref[group]

        def each_block(block, rank):
            slot = slots_ref[video, block]
            mine = (slot // slots_dev == own_group) & (rank < cap)

            @pl.when(mine)
            def _():
                for core in range(2):
                    copy_of(slot - own_group * slots_dev, group, rank, core).start()

            return rank + mine.astype(jnp.int32)

        lax.fori_loop(0, blocks, each_block, jnp.int32(0), unroll=True)
        return carry

    lax.fori_loop(0, groups, each_group, jnp.int32(0))
    for group in range(groups):
        for rank in range(cap):
            for core in range(2):
                copy_of(0, group, rank, core).wait()


def pack(cache, place, slots, videos, cap, head0, heads):
    groups = videos.shape[0]
    width = heads * HD
    half = cache.shape[-1] // 2
    return pl.pallas_call(
        functools.partial(pack_kernel, cap, head0, width, half),
        out_shape=jax.ShapeDtypeStruct((2 * groups, 2, cap, cache.shape[2], width), cache.dtype),
        grid_spec=pltpu.PrefetchScalarGridSpec(
            num_scalar_prefetch=3,
            grid=(1,),
            in_specs=[pl.BlockSpec(memory_space=pl.ANY)],
            out_specs=pl.BlockSpec((2 * groups, 2, cap, cache.shape[2], width), lambda i, *_: (0, 0, 0, 0, 0)),
            scratch_shapes=[pltpu.SemaphoreType.DMA((2 * groups * cap,))],
        ),
        compiler_params=pltpu.CompilerParams(vmem_limit_bytes=VMEM_LIMIT),
        cost_estimate=pl.CostEstimate(flops=0, bytes_accessed=2 * 4 * groups * 2 * cap * cache.shape[2] * width, transcendentals=0),
        name="pack",
    )(place, slots, videos, cache)


def norm_kernel(half, place_ref, qkv_ref, gains_ref, *out_refs):
    core = place_ref[1]

    def normed(which):
        widened = qkv_ref[which].astype(jnp.float32)
        mean_square = jnp.mean(widened * widened, axis=-1, keepdims=True)
        return (widened * lax.rsqrt(mean_square + EPS) * gains_ref[which : which + 1, :]).astype(jnp.bfloat16)

    rows = (normed(0), normed(1), qkv_ref[2])

    def put(own):
        for which in range(3):
            out_refs[2 * which][...] = rows[which][:, own * half : (own + 1) * half]
            out_refs[2 * which + 1][...] = rows[which][:, (1 - own) * half : (2 - own) * half]

    @pl.when(core == 0)
    def _():
        put(0)

    @pl.when(core != 0)
    def _():
        put(1)


def norm(qkv, gains, place):
    _, tokens, width = qkv.shape
    half = width // 2
    block = math.gcd(tokens, 64)
    out = jax.ShapeDtypeStruct((tokens, half), jnp.bfloat16)
    return pl.pallas_call(
        functools.partial(norm_kernel, half),
        out_shape=[out] * 6,
        grid_spec=pltpu.PrefetchScalarGridSpec(
            num_scalar_prefetch=1,
            grid=(tokens // block,),
            in_specs=[
                pl.BlockSpec((3, block, width), lambda i, p: (0, i, 0)),
                pl.BlockSpec((2, width), lambda i, p: (0, 0)),
            ],
            out_specs=[pl.BlockSpec((block, half), lambda i, p: (i, 0))] * 6,
        ),
        compiler_params=pltpu.CompilerParams(vmem_limit_bytes=VMEM_LIMIT),
        cost_estimate=pl.CostEstimate(flops=8 * tokens * width, bytes_accessed=12 * tokens * width, transcendentals=tokens),
        name="norm",
    )(place, qkv, gains)


def attend_kernel(heads, pieces, bias_ref, kc_ref, vc_ref, *refs):
    q_refs = refs[:pieces]
    kn_refs = refs[pieces : pieces + 2]
    vn_refs = refs[pieces + 2 : pieces + 4]
    out_refs = refs[pieces + 4 : 2 * pieces + 4]
    k_ref, v_ref = refs[2 * pieces + 4 :]
    head = pl.program_id(0)
    cached = bias_ref.shape[1]
    tokens = kn_refs[0].shape[0]
    k_ref[:cached] = kc_ref[...].reshape(cached, HD)
    v_ref[:cached] = vc_ref[...].reshape(cached, HD)
    for i in range(2):
        k_ref[cached + i * tokens : cached + (i + 1) * tokens] = kn_refs[i][...]
        v_ref[cached + i * tokens : cached + (i + 1) * tokens] = vn_refs[i][...]
    factor = math.log2(math.e) * HD ** (-0.5)
    lane = lax.broadcasted_iota(jnp.int32, (tokens, HD), 1)
    for q_ref, out_ref in zip(q_refs, out_refs):
        scores = lax.dot_general(q_ref[...], k_ref[...], (((1,), (1,)), ((), ())), preferred_element_type=jnp.float32)
        scores = scores * factor
        scores = jnp.concatenate([scores[:, :cached] + bias_ref[...], scores[:, cached:]], axis=1)
        row_max = jnp.max(scores, axis=-1, keepdims=True)
        weights = jnp.exp2(scores - row_max)
        row_total = jnp.sum(weights, axis=-1, keepdims=True)
        mixed = jnp.dot(weights.astype(jnp.bfloat16), v_ref[...], preferred_element_type=jnp.float32)
        out_ref[:, pl.ds(pl.multiple_of(head * HD, HD), HD)] = (mixed / row_total).astype(jnp.bfloat16)
        level = row_max + jnp.log2(row_total)
        high = level.astype(jnp.bfloat16).astype(jnp.float32)
        middle = (level - high).astype(jnp.bfloat16).astype(jnp.float32)
        low = level - high - middle
        old = jnp.where(head == 0, 0.0, out_ref[:, heads * HD :].astype(jnp.float32))
        new = jnp.where(lane == head, high, old)
        new = jnp.where(lane == head + 32, middle, new)
        new = jnp.where(lane == head + 64, low, new)
        out_ref[:, heads * HD :] = new.astype(jnp.bfloat16)


def attend(bias, arrived, queries, new_keys, new_values, head0, heads):
    pieces = len(queries)
    tokens = queries[0].shape[0]
    sources, _, rows, _ = arrived.shape
    cached = sources * rows
    keys = cached + 2 * tokens
    column = pl.BlockSpec((tokens, HD), lambda h: (0, head0 + h))
    out = jax.ShapeDtypeStruct((tokens, (heads + 1) * HD), jnp.bfloat16)
    work = pieces * tokens * keys * heads
    return pl.pallas_call(
        functools.partial(attend_kernel, heads, pieces),
        out_shape=[out] * pieces,
        grid=(heads,),
        in_specs=[
            pl.BlockSpec((1, cached), lambda h: (0, 0)),
            pl.BlockSpec((sources, None, rows, HD), lambda h: (0, 0, 0, h)),
            pl.BlockSpec((sources, None, rows, HD), lambda h: (0, 1, 0, h)),
        ]
        + [column] * (pieces + 4),
        out_specs=[pl.BlockSpec((tokens, (heads + 1) * HD), lambda h: (0, 0))] * pieces,
        scratch_shapes=[pltpu.VMEM((keys, HD), jnp.bfloat16)] * 2,
        compiler_params=pltpu.CompilerParams(vmem_limit_bytes=VMEM_LIMIT),
        cost_estimate=pl.CostEstimate(flops=4 * HD * work, bytes_accessed=4 * keys * heads * HD + 4 * pieces * tokens * heads * HD, transcendentals=work),
        name="attend",
    )(bias, arrived, arrived, *queries, *new_keys, *new_values)


def merge_kernel(heads, x_count, head0, place_ref, *refs):
    parts = refs[: 2 * x_count]
    whole_ref, joined_ref, sems = refs[-3:]
    half_width = whole_ref.shape[1] // 2
    copies = []
    for side in range(2):
        stats = [parts[dx * 2 + side][:, heads * HD :].astype(jnp.float32) for dx in range(x_count)]
        levels = [stat + pltpu.roll(stat, HD - 32, 1) + pltpu.roll(stat, HD - 64, 1) for stat in stats]
        top = functools.reduce(jnp.maximum, levels)
        shares = [jnp.exp2(level - top) for level in levels]
        total = sum(shares)
        shares = [share / total for share in shares]
        for head in range(heads):
            columns = slice(head * HD, (head + 1) * HD)
            joined = sum(
                shares[dx][:, head : head + 1] * parts[dx * 2 + side][:, columns].astype(jnp.float32)
                for dx in range(x_count)
            )
            joined_ref[side, :, columns] = joined.astype(joined_ref.dtype)
        core = place_ref[1] if side == 0 else 1 - place_ref[1]
        start = pl.multiple_of(core * half_width + head0 * HD, HD)
        copy = pltpu.make_async_copy(joined_ref.at[side], whole_ref.at[:, pl.ds(start, heads * HD)], sems.at[side])
        copy.start()
        copies.append(copy)
    for copy in copies:
        copy.wait()


def merge(parts, place, whole, width, head0, heads):
    tokens = parts[0].shape[0]
    in_specs = [pl.BlockSpec(part.shape, lambda i, *_: (0, 0)) for part in parts]
    operands = list(parts)
    aliases = {}
    if whole is not None:
        in_specs.append(pl.BlockSpec(memory_space=pl.ANY))
        operands.append(whole)
        aliases = {len(operands): 0}
    return pl.pallas_call(
        functools.partial(merge_kernel, heads, len(parts) // 2, head0),
        out_shape=jax.ShapeDtypeStruct((tokens, width), jnp.bfloat16),
        grid_spec=pltpu.PrefetchScalarGridSpec(
            num_scalar_prefetch=1,
            grid=(1,),
            in_specs=in_specs,
            out_specs=pl.BlockSpec(memory_space=pl.ANY),
            scratch_shapes=[pltpu.VMEM((2, tokens, heads * HD), jnp.bfloat16), pltpu.SemaphoreType.DMA((2,))],
        ),
        input_output_aliases=aliases,
        compiler_params=pltpu.CompilerParams(vmem_limit_bytes=VMEM_LIMIT),
        cost_estimate=pl.CostEstimate(flops=8 * tokens * heads * HD * len(parts), bytes_accessed=4 * tokens * heads * HD * len(parts), transcendentals=0),
        name="merge",
    )(place, *operands)


def plan_chunks(heads):
    if sum(CHUNKS) == heads:
        sizes = CHUNKS
    else:
        sizes = (heads,)
    starts = [sum(sizes[:i]) for i in range(len(sizes))]
    return list(zip(starts, sizes))


def body(stretch_qkv, norm_gains, cache, cached_stretches, block_slot, video_of_group):
    x_count = lax.axis_size("x")
    groups = lax.axis_size("rep")
    own_group = lax.axis_index("rep")
    core = lax.axis_index("core")
    place = jnp.stack([own_group, core]).astype(jnp.int32)
    qkv = jnp.transpose(stretch_qkv[0], (1, 0, 2))
    _, tokens, width = qkv.shape
    half = width // 2
    slots_dev, _, block_wide, _ = cache.shape
    cap = slots_dev // groups
    blocks = block_slot.shape[1]
    stretch = tokens * 2 * x_count
    block_len = block_wide * 2 * x_count

    q_own, q_far, k_own, k_far, v_own, v_far = norm(qkv, norm_gains, place)

    def offset_perm(dx, dc, back):
        pairs = []
        for x in range(x_count):
            for c in range(2):
                here, there = x * 2 + c, ((x + dx) % x_count) * 2 + (c + dc) % 2
                pairs.append((there, here) if back else (here, there))
        return pairs

    def move(value, dx, dc, back=False):
        if dx == 0 and dc == 0:
            return value
        return lax.ppermute(value, ("x", "core"), offset_perm(dx, dc, back))

    new_keys = [k_own, move(k_far, 0, 1)]
    new_values = [v_own, move(v_far, 0, 1)]
    offsets = [(dx, dc) for dx in range(x_count) for dc in range(2)]
    queries = [move(q_far if dc else q_own, dx, dc) for dx, dc in offsets]

    own_video = video_of_group[own_group]
    own_slots = block_slot[own_video]
    owners = own_slots // slots_dev
    order = jnp.arange(blocks, dtype=jnp.int32)
    rank = jnp.sum(((owners[:, None] == owners[None, :]) & (order[:, None] > order[None, :])).astype(jnp.int32), axis=1)
    shown = order * block_len < cached_stretches[own_video] * stretch
    unit = owners * cap + rank
    shown_unit = jnp.any((unit[:, None] == jnp.arange(groups * cap)[None, :]) & shown[:, None], axis=0)
    bias = jnp.where(shown_unit, 0.0, -jnp.inf).astype(jnp.float32)
    bias = jnp.broadcast_to(bias[None, :, None], (2, groups * cap, block_wide)).reshape(1, -1)

    chunks = plan_chunks(half // HD)

    def fetch(index, *earlier):
        head0, heads = chunks[index]
        sent = pack(cache, place, block_slot, video_of_group, cap, head0, heads)
        sent = lax.optimization_barrier((sent, *earlier))[0]
        got = lax.all_to_all(sent, ("core", "rep"), split_axis=0, concat_axis=0, tiled=True)
        rows = cap * block_wide
        got = got.reshape(2 * groups, 2, rows, heads * HD)
        if rows % 16:
            got = jnp.transpose(got, (1, 0, 2, 3)).reshape(1, 2, 2 * groups * rows, heads * HD)
        return got

    whole = None
    got = fetch(0)
    held = [q_own, k_own]
    done = []
    for index, (head0, heads) in enumerate(chunks):
        following = fetch(index + 1, got, *held, *done) if index + 1 < len(chunks) else None
        done = [] if whole is None else [whole]
        outs = attend(bias, got, queries, new_keys, new_values, head0, heads)
        held = [outs[0]]
        parts = [move(out, dx, dc, back=True) for out, (dx, dc) in zip(outs, offsets)]
        whole = merge(parts, place, whole, width, head0, heads)
        got = following
    return whole[None]


def solution(mesh):
    wide, rep = mesh.devices.shape
    fine = Mesh(mesh.devices.reshape(wide // 2, 2, rep), ("x", "core", "rep"))
    wide_axes = ("x", "core")
    in_specs = (P("rep", wide_axes, None, None), P(), P("rep", None, wide_axes, None), P(), P(), P())
    out_specs = P("rep", wide_axes, None)
    return jax.shard_map(body, mesh=fine, in_specs=in_specs, out_specs=out_specs, check_vma=False)
```

```python
import functools
import math

import jax
import jax.numpy as jnp
from jax import lax
from jax.experimental import pallas as pl
from jax.experimental.pallas import tpu as pltpu
from jax.sharding import Mesh, PartitionSpec as P

HD = 128
EPS = 1e-06
STAT_ROWS = 16
VMEM_LIMIT = 56 * 1024 * 1024
CHUNKS = (8, 6, 4, 2)


def own_blocks(own_group, slots_ref, videos_ref, slots_dev, visit):
    def each_group(group, carry):
        video = videos_ref[group]

        def each_block(block, rank):
            slot = slots_ref[video, block]
            mine = slot // slots_dev == own_group
            pl.when(mine)(functools.partial(visit, group, rank, slot - own_group * slots_dev))
            return rank + mine.astype(jnp.int32)

        lax.fori_loop(0, slots_ref.shape[1], each_block, jnp.int32(0), unroll=True)
        return carry

    lax.fori_loop(0, videos_ref.shape[0], each_group, jnp.int32(0))


def pack_kernel(cap, head0, width, half, place_ref, slots_ref, videos_ref, cache_ref, out_ref, sems):
    groups = videos_ref.shape[0]

    def copy_of(slot, group, rank, core):
        return pltpu.make_async_copy(
            cache_ref.at[slot, :, :, pl.ds(core * half + head0 * HD, width)],
            out_ref.at[core * groups + group, :, rank],
            sems.at[(group * cap + rank) * 2 + core],
        )

    def visit(group, rank, slot):
        @pl.when(rank < cap)
        def _():
            for core in range(2):
                copy_of(slot, group, rank, core).start()

    own_blocks(place_ref[0], slots_ref, videos_ref, cache_ref.shape[0], visit)
    for group in range(groups):
        for rank in range(cap):
            for core in range(2):
                copy_of(0, group, rank, core).wait()


def pack(cache, place, slots, videos, cap, head0, heads):
    groups = videos.shape[0]
    width = heads * HD
    half = cache.shape[-1] // 2
    shape = (2 * groups, 2, cap, cache.shape[2], width)
    return pl.pallas_call(
        functools.partial(pack_kernel, cap, head0, width, half),
        out_shape=jax.ShapeDtypeStruct(shape, cache.dtype),
        grid_spec=pltpu.PrefetchScalarGridSpec(
            num_scalar_prefetch=3,
            grid=(1,),
            in_specs=[pl.BlockSpec(memory_space=pl.ANY)],
            out_specs=pl.BlockSpec(shape, lambda i, *_: (0, 0, 0, 0, 0)),
            scratch_shapes=[pltpu.SemaphoreType.DMA((2 * groups * cap,))],
        ),
        compiler_params=pltpu.CompilerParams(vmem_limit_bytes=VMEM_LIMIT),
        cost_estimate=pl.CostEstimate(flops=0, bytes_accessed=4 * math.prod(shape), transcendentals=0),
        name="pack",
    )(place, slots, videos, cache)


def norm_kernel(half, place_ref, qkv_ref, gains_ref, *out_refs):
    core = place_ref[1]

    def normed(which):
        widened = qkv_ref[which].astype(jnp.float32)
        mean_square = jnp.mean(widened * widened, axis=-1, keepdims=True)
        return (widened * lax.rsqrt(mean_square + EPS) * gains_ref[which : which + 1, :]).astype(jnp.bfloat16)

    rows = (normed(0), normed(1), qkv_ref[2])

    def put(own):
        for which in range(3):
            out_refs[2 * which][...] = rows[which][:, own * half : (own + 1) * half]
            out_refs[2 * which + 1][...] = rows[which][:, (1 - own) * half : (2 - own) * half]

    @pl.when(core == 0)
    def _():
        put(0)

    @pl.when(core != 0)
    def _():
        put(1)


def norm(qkv, gains, place):
    _, tokens, width = qkv.shape
    half = width // 2
    block = math.gcd(tokens, 64)
    out = jax.ShapeDtypeStruct((tokens, half), jnp.bfloat16)
    return pl.pallas_call(
        functools.partial(norm_kernel, half),
        out_shape=[out] * 6,
        grid_spec=pltpu.PrefetchScalarGridSpec(
            num_scalar_prefetch=1,
            grid=(tokens // block,),
            in_specs=[
                pl.BlockSpec((3, block, width), lambda i, p: (0, i, 0)),
                pl.BlockSpec((2, width), lambda i, p: (0, 0)),
            ],
            out_specs=[pl.BlockSpec((block, half), lambda i, p: (i, 0))] * 6,
        ),
        compiler_params=pltpu.CompilerParams(vmem_limit_bytes=VMEM_LIMIT),
        cost_estimate=pl.CostEstimate(flops=8 * tokens * width, bytes_accessed=12 * tokens * width, transcendentals=tokens),
        name="norm",
    )(place, qkv, gains)


def attend_kernel(heads, pieces, bias_ref, kc_ref, vc_ref, *refs):
    q_refs = refs[:pieces]
    kn_refs = refs[pieces : pieces + 2]
    vn_refs = refs[pieces + 2 : pieces + 4]
    out_refs = refs[pieces + 4 : 2 * pieces + 4]
    k_ref, v_ref = refs[2 * pieces + 4 :]
    head = pl.program_id(0)
    cached = bias_ref.shape[1]
    tokens = kn_refs[0].shape[0]

    @pl.when(head == 0)
    def _():
        v_ref[:, HD:] = jnp.ones_like(v_ref[:, HD:])

    def put(at, rows, keys, values):
        k_ref[at : at + rows, :HD] = keys
        k_ref[at : at + rows, HD:] = keys
        v_ref[at : at + rows, :HD] = values

    put(0, cached, kc_ref[...].reshape(cached, HD), vc_ref[...].reshape(cached, HD))
    at = cached
    for i in range(2):
        put(at, tokens, kn_refs[i][...], vn_refs[i][...])
        at += tokens
    factor = math.log2(math.e) * HD ** (-0.5)
    segment = tokens // 3
    row = lax.broadcasted_iota(jnp.int32, (STAT_ROWS, HD), 0)

    def scores_of(q_ref):
        scaled = q_ref[...].astype(jnp.float32) * factor
        high = scaled.astype(jnp.bfloat16)
        low = (scaled - high.astype(jnp.float32)).astype(jnp.bfloat16)
        query = jnp.concatenate([high, low], axis=1)
        return lax.dot_general(query, k_ref[...], (((1,), (1,)), ((), ())), preferred_element_type=jnp.float32)

    def finish(scores, out_ref):
        scores = jnp.concatenate([scores[:, :cached] + bias_ref[...], scores[:, cached:]], axis=1)
        row_max = jnp.max(scores, axis=-1, keepdims=True)
        weights = jnp.exp2(scores - row_max).astype(jnp.bfloat16)
        mixed = jnp.dot(weights, v_ref[...], preferred_element_type=jnp.float32)
        row_total = mixed[:, HD:]
        columns = pl.ds(pl.multiple_of(head * HD, HD), HD)
        out_ref[:tokens, columns] = (mixed[:, :HD] / row_total).astype(jnp.bfloat16)
        level = row_max + jnp.log2(row_total)
        tile = jnp.zeros((STAT_ROWS, HD), jnp.float32)
        for part in range(3):
            flat = jnp.transpose(level[part * segment : (part + 1) * segment])[:STAT_ROWS]
            if segment < HD:
                flat = jnp.concatenate([flat, jnp.zeros((STAT_ROWS, HD - segment), jnp.float32)], axis=1)
            high = flat.astype(jnp.bfloat16).astype(jnp.float32)
            middle = (flat - high).astype(jnp.bfloat16).astype(jnp.float32)
            tile = jnp.where(row == part, high, tile)
            tile = jnp.where(row == 3 + part, middle, tile)
            tile = jnp.where(row == 6 + part, flat - high - middle, tile)
        out_ref[tokens:, columns] = tile.astype(jnp.bfloat16)

    scores = scores_of(q_refs[0])
    for i in range(pieces):
        following = scores_of(q_refs[i + 1]) if i + 1 < pieces else None
        finish(scores, out_refs[i])
        scores = following


def attend(bias, arrived, queries, new_keys, new_values, head0, heads):
    pieces = len(queries)
    tokens = queries[0][0].shape[0]
    cached = bias.shape[1]
    keys = cached + 2 * tokens
    sources, _, rows, _ = arrived.shape

    def column(first):
        return pl.BlockSpec((tokens, HD), lambda h: (0, head0 - first + h))

    in_specs = [
        pl.BlockSpec((1, cached), lambda h: (0, 0)),
        pl.BlockSpec((sources, None, rows, HD), lambda h: (0, 0, 0, h)),
        pl.BlockSpec((sources, None, rows, HD), lambda h: (0, 1, 0, h)),
    ]
    operands = [bias, arrived, arrived]
    for array, first in queries:
        in_specs.append(column(first))
        operands.append(array)
    for array in (*new_keys, *new_values):
        in_specs.append(column(0))
        operands.append(array)
    out = jax.ShapeDtypeStruct((tokens + STAT_ROWS, heads * HD), jnp.bfloat16)
    work = pieces * tokens * keys * heads
    return pl.pallas_call(
        functools.partial(attend_kernel, heads, pieces),
        out_shape=[out] * pieces,
        grid=(heads,),
        in_specs=in_specs,
        out_specs=[pl.BlockSpec((tokens + STAT_ROWS, heads * HD), lambda h: (0, 0))] * pieces,
        scratch_shapes=[pltpu.VMEM((keys, 2 * HD), jnp.bfloat16)] * 2,
        compiler_params=pltpu.CompilerParams(vmem_limit_bytes=VMEM_LIMIT),
        cost_estimate=pl.CostEstimate(flops=8 * HD * work, bytes_accessed=4 * keys * heads * HD + 4 * pieces * tokens * heads * HD, transcendentals=work),
        name="attend",
    )(*operands)


def merge_kernel(heads, x_count, head0, place_ref, *refs):
    parts = refs[: 2 * x_count]
    whole_ref, joined_ref, sems = refs[-3:]
    half_width = whole_ref.shape[1] // 2
    tokens = whole_ref.shape[0]
    segment = tokens // 3
    row = lax.broadcasted_iota(jnp.int32, (STAT_ROWS, HD), 0)
    copies = []
    for side in range(2):
        for head in range(heads):
            columns = slice(head * HD, (head + 1) * HD)
            for part in range(3):
                own = (row == part) | (row == 3 + part) | (row == 6 + part)
                rows = slice(part * segment, (part + 1) * segment)
                levels = [
                    lax.dot_general(
                        parts[dx * 2 + side][tokens:, columns][:, :segment],
                        own.astype(jnp.bfloat16),
                        (((0,), (0,)), ((), ())),
                        preferred_element_type=jnp.float32,
                    )
                    for dx in range(x_count)
                ]
                top = functools.reduce(jnp.maximum, levels)
                shares = [jnp.exp2(level - top) for level in levels]
                total = sum(shares)
                joined = sum(
                    shares[dx] * parts[dx * 2 + side][rows, columns].astype(jnp.float32) for dx in range(x_count)
                )
                joined_ref[side, rows, columns] = (joined / total).astype(joined_ref.dtype)
        core = place_ref[1] if side == 0 else 1 - place_ref[1]
        start = pl.multiple_of(core * half_width + head0 * HD, HD)
        copy = pltpu.make_async_copy(joined_ref.at[side], whole_ref.at[:, pl.ds(start, heads * HD)], sems.at[side])
        copy.start()
        copies.append(copy)
    for copy in copies:
        copy.wait()


def merge(parts, place, whole, width, head0, heads):
    tokens = parts[0].shape[0] - STAT_ROWS
    in_specs = [pl.BlockSpec(part.shape, lambda i, *_: (0, 0)) for part in parts]
    operands = list(parts)
    aliases = {}
    if whole is not None:
        in_specs.append(pl.BlockSpec(memory_space=pl.ANY))
        operands.append(whole)
        aliases = {len(operands): 0}
    return pl.pallas_call(
        functools.partial(merge_kernel, heads, len(parts) // 2, head0),
        out_shape=jax.ShapeDtypeStruct((tokens, width), jnp.bfloat16),
        grid_spec=pltpu.PrefetchScalarGridSpec(
            num_scalar_prefetch=1,
            grid=(1,),
            in_specs=in_specs,
            out_specs=pl.BlockSpec(memory_space=pl.ANY),
            scratch_shapes=[pltpu.VMEM((2, tokens, heads * HD), jnp.bfloat16), pltpu.SemaphoreType.DMA((2,))],
        ),
        input_output_aliases=aliases,
        compiler_params=pltpu.CompilerParams(vmem_limit_bytes=VMEM_LIMIT),
        cost_estimate=pl.CostEstimate(flops=8 * tokens * heads * HD * len(parts), bytes_accessed=4 * tokens * heads * HD * len(parts), transcendentals=0),
        name="merge",
    )(place, *operands)


def plan_chunks(heads):
    sizes = CHUNKS if sum(CHUNKS) == heads else (heads,)
    starts = [sum(sizes[:i]) for i in range(len(sizes))]
    return list(zip(starts, sizes))


def body(stretch_qkv, norm_gains, cache, cached_stretches, block_slot, video_of_group):
    x_count = lax.axis_size("x")
    groups = lax.axis_size("rep")
    own_group = lax.axis_index("rep")
    core = lax.axis_index("core")
    place = jnp.stack([own_group, core]).astype(jnp.int32)
    qkv = jnp.transpose(stretch_qkv[0], (1, 0, 2))
    _, tokens, width = qkv.shape
    half = width // 2
    slots_dev, _, block_wide, _ = cache.shape
    cap = slots_dev // groups
    blocks = block_slot.shape[1]
    stretch = tokens * 2 * x_count
    block_len = block_wide * 2 * x_count
    chunks = plan_chunks(half // HD)
    offsets = [(dx, dc) for dx in range(x_count) for dc in range(2)]

    def move(value, dx, dc, back=False):
        if dx == 0 and dc == 0:
            return value
        pairs = []
        for x in range(x_count):
            for c in range(2):
                here, there = x * 2 + c, ((x + dx) % x_count) * 2 + (c + dc) % 2
                pairs.append((there, here) if back else (here, there))
        return lax.ppermute(value, ("x", "core"), pairs)

    def tie(value, *others):
        return lax.optimization_barrier((value, *others))[0]

    def spread_out(index, *earlier):
        head0, heads = chunks[index]
        sent = pack(cache, place, block_slot, video_of_group, cap, head0, heads)
        if earlier:
            sent = tie(sent, *earlier)
        got = lax.all_to_all(sent, ("core", "rep"), split_axis=0, concat_axis=0, tiled=True)
        rows = cap * block_wide
        got = got.reshape(2 * groups, 2, rows, heads * HD)
        if rows % 16:
            got = jnp.transpose(got, (1, 0, 2, 3)).reshape(1, 2, 2 * groups * rows, heads * HD)
        return got

    got = spread_out(0)

    own_video = video_of_group[own_group]
    own_slots = block_slot[own_video]
    owners = own_slots // slots_dev
    order = jnp.arange(blocks, dtype=jnp.int32)
    rank = jnp.sum(((owners[:, None] == owners[None, :]) & (order[:, None] > order[None, :])).astype(jnp.int32), axis=1)
    shown = order * block_len < cached_stretches[own_video] * stretch
    unit = owners * cap + rank
    shown_unit = jnp.any((unit[:, None] == jnp.arange(groups * cap)[None, :]) & shown[:, None], axis=0)
    bias = jnp.where(shown_unit, 0.0, -jnp.inf).astype(jnp.float32)
    bias = jnp.broadcast_to(bias[None, :, None], (2, groups * cap, block_wide)).reshape(1, -1)

    q_own, q_far, k_own, k_far, v_own, v_far = norm(qkv, norm_gains, place)
    new_keys = [k_own, move(k_far, 0, 1)]
    new_values = [v_own, move(v_far, 0, 1)]
    early = chunks[0][1]
    early_queries = [move((q_far if dc else q_own)[:, : early * HD], dx, dc) for dx, dc in offsets]
    late_queries = []
    if len(chunks) > 1:
        late_queries = [move((q_far if dc else q_own)[:, early * HD :], dx, dc) for dx, dc in offsets]

    wholes = []
    held, done = [*early_queries, new_keys[1], new_values[1]], []
    for index, (head0, heads) in enumerate(chunks):
        last = index + 1 == len(chunks)
        following = None if last else spread_out(index + 1, got, *held, *done)
        queries = [(array, early if index else 0) for array in (late_queries if index else early_queries)]
        near = pieces = len(offsets)
        if last and len(chunks) > 2:
            near = 2
            got = tie(got, wholes[-2])
        far_outs = attend(bias, got, queries[near:], new_keys, new_values, head0, heads) if near < pieces else []
        own_outs = attend(bias, got, queries[:near], new_keys, new_values, head0, heads)
        outs = [*own_outs, *far_outs]
        parts = [move(out, dx, dc, back=True) for out, (dx, dc) in zip(outs, offsets)]
        done = wholes[-1:]
        wholes.append(merge(parts, place, wholes[-1] if wholes else None, width, head0, heads))
        held = parts + (late_queries if index == 0 else [])
        got = following
    return wholes[-1][None]


def solution(mesh):
    wide, rep = mesh.devices.shape
    fine = Mesh(mesh.devices.reshape(wide // 2, 2, rep), ("x", "core", "rep"))
    wide_axes = ("x", "core")
    in_specs = (P("rep", wide_axes, None, None), P(), P("rep", None, wide_axes, None), P(), P(), P())
    out_specs = P("rep", wide_axes, None)
    return jax.shard_map(body, mesh=fine, in_specs=in_specs, out_specs=out_specs, check_vma=False)
```

```python
import functools
import math

import jax
import jax.numpy as jnp
from jax import lax
from jax.experimental import pallas as pl
from jax.experimental.pallas import tpu as pltpu
from jax.sharding import Mesh, PartitionSpec as P

HD = 128
EPS = 1e-06
STAT_ROWS = 16
VMEM_LIMIT = 56 * 1024 * 1024
CHUNKS = (8, 6, 4, 2)


def own_blocks(own_group, slots_ref, videos_ref, slots_dev, visit):
    def each_group(group, carry):
        video = videos_ref[group]

        def each_block(block, rank):
            slot = slots_ref[video, block] - own_group * slots_dev
            mine = (slot >= 0) & (slot < slots_dev)
            pl.when(mine)(functools.partial(visit, group, rank, slot))
            return rank + mine.astype(jnp.int32)

        lax.fori_loop(0, slots_ref.shape[1], each_block, jnp.int32(0), unroll=True)
        return carry

    lax.fori_loop(0, videos_ref.shape[0], each_group, jnp.int32(0))


def pack_kernel(cap, head0, width, half, place_ref, slots_ref, videos_ref, cache_ref, out_ref, held_ref, in_sems, out_sems):
    groups = videos_ref.shape[0]

    def copy_in(slot, group, rank, core):
        return pltpu.make_async_copy(
            cache_ref.at[slot, :, :, pl.ds(core * half + head0 * HD, width)],
            held_ref.at[core * groups + group, :, rank],
            in_sems.at[(group * cap + rank) * 2 + core],
        )

    def copy_out(group, core):
        at = core * groups + group
        return pltpu.make_async_copy(held_ref.at[at], out_ref.at[at], out_sems.at[at])

    def visit(group, rank, slot):
        @pl.when(rank < cap)
        def _():
            for core in range(2):
                copy_in(slot, group, rank, core).start()

    own_blocks(place_ref[0], slots_ref, videos_ref, cache_ref.shape[0], visit)
    for group in range(groups):
        for core in range(2):
            for rank in range(cap):
                copy_in(0, group, rank, core).wait()
            copy_out(group, core).start()
    for group in range(groups):
        for core in range(2):
            copy_out(group, core).wait()


def pack(cache, place, slots, videos, cap, head0, heads):
    groups = videos.shape[0]
    width = heads * HD
    half = cache.shape[-1] // 2
    shape = (2 * groups, 2, cap, cache.shape[2], width)
    return pl.pallas_call(
        functools.partial(pack_kernel, cap, head0, width, half),
        out_shape=jax.ShapeDtypeStruct(shape, cache.dtype),
        grid_spec=pltpu.PrefetchScalarGridSpec(
            num_scalar_prefetch=3,
            grid=(1,),
            in_specs=[pl.BlockSpec(memory_space=pl.ANY)],
            out_specs=pl.BlockSpec(memory_space=pl.ANY),
            scratch_shapes=[
                pltpu.VMEM(shape, cache.dtype),
                pltpu.SemaphoreType.DMA((2 * groups * cap,)),
                pltpu.SemaphoreType.DMA((2 * groups,)),
            ],
        ),
        compiler_params=pltpu.CompilerParams(vmem_limit_bytes=VMEM_LIMIT),
        cost_estimate=pl.CostEstimate(flops=0, bytes_accessed=4 * math.prod(shape), transcendentals=0),
        name="pack",
    )(place, slots, videos, cache)


def norm_kernel(half, place_ref, qkv_ref, gains_ref, *out_refs):
    core = place_ref[1]

    def normed(which):
        widened = qkv_ref[which].astype(jnp.float32)
        mean_square = jnp.mean(widened * widened, axis=-1, keepdims=True)
        return (widened * lax.rsqrt(mean_square + EPS) * gains_ref[which : which + 1, :]).astype(jnp.bfloat16)

    rows = (normed(0), normed(1), qkv_ref[2])

    def put(own):
        for which in range(3):
            out_refs[2 * which][...] = rows[which][:, own * half : (own + 1) * half]
            out_refs[2 * which + 1][...] = rows[which][:, (1 - own) * half : (2 - own) * half]

    @pl.when(core == 0)
    def _():
        put(0)

    @pl.when(core != 0)
    def _():
        put(1)


def norm(qkv, gains, place):
    _, tokens, width = qkv.shape
    half = width // 2
    block = math.gcd(tokens, 64)
    out = jax.ShapeDtypeStruct((tokens, half), jnp.bfloat16)
    return pl.pallas_call(
        functools.partial(norm_kernel, half),
        out_shape=[out] * 6,
        grid_spec=pltpu.PrefetchScalarGridSpec(
            num_scalar_prefetch=1,
            grid=(tokens // block,),
            in_specs=[
                pl.BlockSpec((3, block, width), lambda i, p: (0, i, 0)),
                pl.BlockSpec((2, width), lambda i, p: (0, 0)),
            ],
            out_specs=[pl.BlockSpec((block, half), lambda i, p: (i, 0))] * 6,
        ),
        compiler_params=pltpu.CompilerParams(vmem_limit_bytes=VMEM_LIMIT),
        cost_estimate=pl.CostEstimate(flops=8 * tokens * width, bytes_accessed=12 * tokens * width, transcendentals=tokens),
        name="norm",
    )(place, qkv, gains)


def attend_kernel(heads, pieces, bias_ref, kc_ref, vc_ref, *refs):
    q_refs = refs[:pieces]
    kn_refs = refs[pieces : pieces + 2]
    vn_refs = refs[pieces + 2 : pieces + 4]
    out_refs = refs[pieces + 4 : 2 * pieces + 4]
    k_ref, v_ref = refs[2 * pieces + 4 :]
    head = pl.program_id(0)
    cached = bias_ref.shape[1]
    tokens = kn_refs[0].shape[0]

    @pl.when(head == 0)
    def _():
        v_ref[:, HD:] = jnp.ones_like(v_ref[:, HD:])

    def put(at, rows, keys, values):
        k_ref[at : at + rows, :HD] = keys
        k_ref[at : at + rows, HD:] = keys
        v_ref[at : at + rows, :HD] = values

    put(0, cached, kc_ref[...].reshape(cached, HD), vc_ref[...].reshape(cached, HD))
    at = cached
    for i in range(2):
        put(at, tokens, kn_refs[i][...], vn_refs[i][...])
        at += tokens
    factor = math.log2(math.e) * HD ** (-0.5)
    segment = tokens // 3
    row = lax.broadcasted_iota(jnp.int32, (STAT_ROWS, HD), 0)

    def scores_of(q_ref):
        scaled = q_ref[...].astype(jnp.float32) * factor
        high = scaled.astype(jnp.bfloat16)
        low = (scaled - high.astype(jnp.float32)).astype(jnp.bfloat16)
        query = jnp.concatenate([high, low], axis=1)
        return lax.dot_general(query, k_ref[...], (((1,), (1,)), ((), ())), preferred_element_type=jnp.float32)

    def finish(scores, out_ref):
        scores = jnp.concatenate([scores[:, :cached] + bias_ref[...], scores[:, cached:]], axis=1)
        row_max = jnp.max(scores, axis=-1, keepdims=True)
        weights = jnp.exp2(scores - row_max).astype(jnp.bfloat16)
        mixed = jnp.dot(weights, v_ref[...], preferred_element_type=jnp.float32)
        row_total = mixed[:, HD:]
        columns = pl.ds(pl.multiple_of(head * HD, HD), HD)
        out_ref[:tokens, columns] = (mixed[:, :HD] / row_total).astype(jnp.bfloat16)
        level = row_max + jnp.log2(row_total)
        tile = jnp.zeros((STAT_ROWS, HD), jnp.float32)
        for part in range(3):
            flat = jnp.transpose(level[part * segment : (part + 1) * segment])[:STAT_ROWS]
            if segment < HD:
                flat = jnp.concatenate([flat, jnp.zeros((STAT_ROWS, HD - segment), jnp.float32)], axis=1)
            high = flat.astype(jnp.bfloat16).astype(jnp.float32)
            middle = (flat - high).astype(jnp.bfloat16).astype(jnp.float32)
            tile = jnp.where(row == part, high, tile)
            tile = jnp.where(row == 3 + part, middle, tile)
            tile = jnp.where(row == 6 + part, flat - high - middle, tile)
        out_ref[tokens:, columns] = tile.astype(jnp.bfloat16)

    scores = scores_of(q_refs[0])
    for i in range(pieces):
        following = scores_of(q_refs[i + 1]) if i + 1 < pieces else None
        finish(scores, out_refs[i])
        scores = following


def attend(bias, arrived, queries, new_keys, new_values, head0, heads):
    pieces = len(queries)
    tokens = queries[0][0].shape[0]
    cached = bias.shape[1]
    keys = cached + 2 * tokens
    sources, _, rows, _ = arrived.shape

    def column(first):
        return pl.BlockSpec((tokens, HD), lambda h: (0, head0 - first + h))

    in_specs = [
        pl.BlockSpec((1, cached), lambda h: (0, 0)),
        pl.BlockSpec((sources, None, rows, HD), lambda h: (0, 0, 0, h)),
        pl.BlockSpec((sources, None, rows, HD), lambda h: (0, 1, 0, h)),
    ]
    operands = [bias, arrived, arrived]
    for array, first in queries:
        in_specs.append(column(first))
        operands.append(array)
    for array in (*new_keys, *new_values):
        in_specs.append(column(0))
        operands.append(array)
    out = jax.ShapeDtypeStruct((tokens + STAT_ROWS, heads * HD), jnp.bfloat16)
    work = pieces * tokens * keys * heads
    return pl.pallas_call(
        functools.partial(attend_kernel, heads, pieces),
        out_shape=[out] * pieces,
        grid=(heads,),
        in_specs=in_specs,
        out_specs=[pl.BlockSpec((tokens + STAT_ROWS, heads * HD), lambda h: (0, 0))] * pieces,
        scratch_shapes=[pltpu.VMEM((keys, 2 * HD), jnp.bfloat16)] * 2,
        compiler_params=pltpu.CompilerParams(vmem_limit_bytes=VMEM_LIMIT),
        cost_estimate=pl.CostEstimate(flops=8 * HD * work, bytes_accessed=4 * keys * heads * HD + 4 * pieces * tokens * heads * HD, transcendentals=work),
        name="attend",
    )(*operands)


def merge_kernel(heads, x_count, head0, place_ref, *refs):
    parts = refs[: 2 * x_count]
    whole_ref, joined_ref, sems = refs[-3:]
    half_width = whole_ref.shape[1] // 2
    tokens = whole_ref.shape[0]
    segment = tokens // 3
    row = lax.broadcasted_iota(jnp.int32, (STAT_ROWS, HD), 0)
    copies = []
    for side in range(2):
        for head in range(heads):
            columns = slice(head * HD, (head + 1) * HD)
            for part in range(3):
                own = (row == part) | (row == 3 + part) | (row == 6 + part)
                rows = slice(part * segment, (part + 1) * segment)
                levels = [
                    lax.dot_general(
                        parts[dx * 2 + side][tokens:, columns][:, :segment],
                        own.astype(jnp.bfloat16),
                        (((0,), (0,)), ((), ())),
                        preferred_element_type=jnp.float32,
                    )
                    for dx in range(x_count)
                ]
                top = functools.reduce(jnp.maximum, levels)
                shares = [jnp.exp2(level - top) for level in levels]
                total = sum(shares)
                joined = sum(
                    shares[dx] * parts[dx * 2 + side][rows, columns].astype(jnp.float32) for dx in range(x_count)
                )
                joined_ref[side, rows, columns] = (joined / total).astype(joined_ref.dtype)
        core = place_ref[1] if side == 0 else 1 - place_ref[1]
        start = pl.multiple_of(core * half_width + head0 * HD, HD)
        copy = pltpu.make_async_copy(joined_ref.at[side], whole_ref.at[:, pl.ds(start, heads * HD)], sems.at[side])
        copy.start()
        copies.append(copy)
    for copy in copies:
        copy.wait()


def merge(parts, place, whole, width, head0, heads):
    tokens = parts[0].shape[0] - STAT_ROWS
    in_specs = [pl.BlockSpec(part.shape, lambda i, *_: (0, 0)) for part in parts]
    operands = list(parts)
    aliases = {}
    if whole is not None:
        in_specs.append(pl.BlockSpec(memory_space=pl.ANY))
        operands.append(whole)
        aliases = {len(operands): 0}
    return pl.pallas_call(
        functools.partial(merge_kernel, heads, len(parts) // 2, head0),
        out_shape=jax.ShapeDtypeStruct((tokens, width), jnp.bfloat16),
        grid_spec=pltpu.PrefetchScalarGridSpec(
            num_scalar_prefetch=1,
            grid=(1,),
            in_specs=in_specs,
            out_specs=pl.BlockSpec(memory_space=pl.ANY),
            scratch_shapes=[pltpu.VMEM((2, tokens, heads * HD), jnp.bfloat16), pltpu.SemaphoreType.DMA((2,))],
        ),
        input_output_aliases=aliases,
        compiler_params=pltpu.CompilerParams(vmem_limit_bytes=VMEM_LIMIT),
        cost_estimate=pl.CostEstimate(flops=8 * tokens * heads * HD * len(parts), bytes_accessed=4 * tokens * heads * HD * len(parts), transcendentals=0),
        name="merge",
    )(place, *operands)


def plan_chunks(heads):
    sizes = CHUNKS if sum(CHUNKS) == heads else (heads,)
    starts = [sum(sizes[:i]) for i in range(len(sizes))]
    return list(zip(starts, sizes))


def body(stretch_qkv, norm_gains, cache, cached_stretches, block_slot, video_of_group):
    x_count = lax.axis_size("x")
    groups = lax.axis_size("rep")
    own_group = lax.axis_index("rep")
    core = lax.axis_index("core")
    place = jnp.stack([own_group, core]).astype(jnp.int32)
    qkv = jnp.transpose(stretch_qkv[0], (1, 0, 2))
    _, tokens, width = qkv.shape
    half = width // 2
    slots_dev, _, block_wide, _ = cache.shape
    cap = slots_dev // groups
    blocks = block_slot.shape[1]
    stretch = tokens * 2 * x_count
    block_len = block_wide * 2 * x_count
    chunks = plan_chunks(half // HD)
    offsets = [(dx, dc) for dx in range(x_count) for dc in range(2)]

    def move(value, dx, dc, back=False):
        if dx == 0 and dc == 0:
            return value
        pairs = []
        for x in range(x_count):
            for c in range(2):
                here, there = x * 2 + c, ((x + dx) % x_count) * 2 + (c + dc) % 2
                pairs.append((there, here) if back else (here, there))
        return lax.ppermute(value, ("x", "core"), pairs)

    def tie(value, *others):
        return lax.optimization_barrier((value, *others))[0]

    def spread_out(index, *earlier):
        head0, heads = chunks[index]
        sent = pack(cache, place, block_slot, video_of_group, cap, head0, heads)
        if earlier:
            sent = tie(sent, *earlier)
        got = lax.all_to_all(sent, ("core", "rep"), split_axis=0, concat_axis=0, tiled=True)
        rows = cap * block_wide
        got = got.reshape(2 * groups, 2, rows, heads * HD)
        if rows % 16:
            got = jnp.transpose(got, (1, 0, 2, 3)).reshape(1, 2, 2 * groups * rows, heads * HD)
        return got

    got = spread_out(0)

    own_video = video_of_group[own_group]
    own_slots = block_slot[own_video]
    owners = own_slots // slots_dev
    order = jnp.arange(blocks, dtype=jnp.int32)
    rank = jnp.sum(((owners[:, None] == owners[None, :]) & (order[:, None] > order[None, :])).astype(jnp.int32), axis=1)
    shown = order * block_len < cached_stretches[own_video] * stretch
    unit = owners * cap + rank
    shown_unit = jnp.any((unit[:, None] == jnp.arange(groups * cap)[None, :]) & shown[:, None], axis=0)
    bias = jnp.where(shown_unit, 0.0, -jnp.inf).astype(jnp.float32)
    bias = jnp.broadcast_to(bias[None, :, None], (2, groups * cap, block_wide)).reshape(1, -1)

    q_own, q_far, k_own, k_far, v_own, v_far = norm(qkv, norm_gains, place)
    new_keys = [k_own, move(k_far, 0, 1)]
    new_values = [v_own, move(v_far, 0, 1)]
    early = chunks[0][1]
    early_queries = [move((q_far if dc else q_own)[:, : early * HD], dx, dc) for dx, dc in offsets]
    late_queries = []
    if len(chunks) > 1:
        late_queries = [move((q_far if dc else q_own)[:, early * HD :], dx, dc) for dx, dc in offsets]

    wholes = []
    held, done = [*early_queries, new_keys[1], new_values[1]], []
    for index, (head0, heads) in enumerate(chunks):
        last = index + 1 == len(chunks)
        following = None if last else spread_out(index + 1, got, *held, *done)
        queries = [(array, early if index else 0) for array in (late_queries if index else early_queries)]
        near = pieces = len(offsets)
        if last and len(chunks) > 2:
            near = 2
            got = tie(got, wholes[-2])
        far_outs = attend(bias, got, queries[near:], new_keys, new_values, head0, heads) if near < pieces else []
        own_outs = attend(bias, got, queries[:near], new_keys, new_values, head0, heads)
        outs = [*own_outs, *far_outs]
        parts = [move(out, dx, dc, back=True) for out, (dx, dc) in zip(outs, offsets)]
        done = wholes[-1:]
        wholes.append(merge(parts, place, wholes[-1] if wholes else None, width, head0, heads))
        held = parts + (late_queries if index == 0 else [])
        got = following
    return wholes[-1][None]


def solution(mesh):
    wide, rep = mesh.devices.shape
    fine = Mesh(mesh.devices.reshape(wide // 2, 2, rep), ("x", "core", "rep"))
    wide_axes = ("x", "core")
    in_specs = (P("rep", wide_axes, None, None), P(), P("rep", None, wide_axes, None), P(), P(), P())
    out_specs = P("rep", wide_axes, None)
    return jax.shard_map(body, mesh=fine, in_specs=in_specs, out_specs=out_specs, check_vma=False)
```
